256 devices in a mesh: ctx: 32 (over x, z), tp: 8 (over y, core).
Axes of the slice: x: 4, y: 4, z: 8, core: 2. Of those that a mesh axis runs over, the one named last changes fastest.
Arguments:
- ctx_q: bfloat16 [32768, 8192], P('ctx', 'tp'), may hold values from -6 to 6
- ctx_k: bfloat16 [32768, 1024], P('ctx', 'tp'), may hold values from -6 to 6
- ctx_v: bfloat16 [32768, 1024], P('ctx', 'tp'), may hold values from -6 to 6
- tail_q: bfloat16 [512, 8192], P('ctx', 'tp'), may hold values from -6 to 6
- tail_k: bfloat16 [512, 1024], P('ctx', 'tp'), may hold values from -6 to 6
- tail_v: bfloat16 [512, 1024], P('ctx', 'tp'), may hold values from -6 to 6
- out_weight: bfloat16 [8192, 8192], P('tp', 'ctx'), may hold values from -0.0625 to 0.0625
Outputs:
- context_out: bfloat16 [32768, 8192], P('ctx', 'tp')
- tail_attn: bfloat16 [512, 8192], P('ctx', 'tp')
- tail_proj: float32 [512, 8192], P('tp', 'ctx')
The draws below stay inside these ranges and needn't reach their ends.
All inputs are finite; a program needn't handle non-finite values.
Results may differ from the reference program's by a relative error of at most 0.0034.
Values may be sent and summed in bfloat16 or wider, within the bound.
A program may use at most 128 MiB of HBM per device.

```python
import jax
import jax.numpy as jnp
from jax import lax

D = 8192
HQ = 64
KVH = 8
HD = 128
BLK = 1024
TAIL = 512
CTX_TOKENS = 32768
N_CTX = 32


def draw_ctx_k(key, part):
    key = jax.random.fold_in(key, 11)
    shape = (CTX_TOKENS, KVH * HD)
    base = jnp.clip(1.5 * jax.random.normal(key, shape, jnp.float32), -6.0, 6.0)
    return base.astype(jnp.bfloat16)


def draw_ctx_q(key, part):
    key = jax.random.fold_in(key, 12)
    shape = (CTX_TOKENS, HQ * HD)
    base = jnp.clip(1.5 * jax.random.normal(key, shape, jnp.float32), -6.0, 6.0)
    return base.astype(jnp.bfloat16)


def draw_tail_q(key, part):
    key = jax.random.fold_in(key, 13)
    shape = (TAIL, HQ * HD)
    base = jnp.clip(1.5 * jax.random.normal(key, shape, jnp.float32), -6.0, 6.0)
    return base.astype(jnp.bfloat16)


def block_levels(own_key, extent, cuts, low, largest):
    loudness, own = 1.0, jax.random.fold_in(own_key, 6)
    for axis_at, parts in cuts:
        draws = jnp.exp(jax.random.uniform(jax.random.fold_in(own, axis_at), (parts,), jnp.float32, low / len(cuts), largest / len(cuts)))
        loudness = loudness * jnp.repeat(draws, extent[axis_at] // parts).reshape([-1 if axis == axis_at else 1 for axis in range(len(extent))])
    return loudness


def scatter_about(stream_key, dims, width, bound, split=(), held_as=jnp.bfloat16):
    values = width * jax.random.normal(stream_key, dims, jnp.float32)
    if split:
        values = values * block_levels(stream_key, dims, split, -0.22, 0.18)
    return jnp.clip(values, -bound, bound).astype(held_as)


def setup_inputs(seed: int = 0) -> dict:
    keys = jax.random.split(jax.random.key(seed), 8)
    ctx_q = draw_ctx_q(jax.random.fold_in(keys[7], 71), 0)
    ctx_k = draw_ctx_k(jax.random.fold_in(keys[7], 71), 0)
    ctx_v = scatter_about(keys[2], (CTX_TOKENS, KVH * HD), 1.0, 6.0, ((0, 32), (1, 8)))
    tail_q = draw_tail_q(jax.random.fold_in(keys[7], 71), 0)
    tail_k = scatter_about(keys[4], (TAIL, KVH * HD), 1.5, 6.0, ((0, 32), (1, 8)))
    tail_v = scatter_about(keys[5], (TAIL, KVH * HD), 1.0, 6.0, ((0, 32), (1, 8)))
    out_weight = scatter_about(keys[6], (HQ * HD, D), (HQ * HD) ** -0.5, 0.0625, ((0, 8), (1, 32)))
    return {"ctx_q": ctx_q, "ctx_k": ctx_k, "ctx_v": ctx_v, "tail_q": tail_q, "tail_k": tail_k, "tail_v": tail_v, "out_weight": out_weight}


def partials(queries, key_rows, value_rows, visible):
    scores = jnp.einsum("rkgd,skd->kgrs", queries.astype(jnp.float32), key_rows.astype(jnp.float32)) * (HD ** -0.5)
    scores = jnp.where(visible[None, None], scores, -jnp.inf)
    best_score = jnp.max(scores, axis=3)
    weights = jnp.exp(scores - best_score[..., None])
    weight_sum = jnp.sum(weights, axis=3)
    rounded = lax.optimization_barrier(weights.astype(jnp.bfloat16))
    weighted = jnp.einsum("kgrs,skd->rkgd", rounded.astype(jnp.float32), value_rows.astype(jnp.float32))
    return best_score, weight_sum, weighted


def reference(ctx_q, ctx_k, ctx_v, tail_q, tail_k, tail_v, out_weight):
    groups = HQ // KVH
    tail_block = TAIL // N_CTX
    ctx_queries = ctx_q.reshape(N_CTX, BLK, KVH, groups, HD)
    ctx_keys = ctx_k.reshape(N_CTX, BLK, KVH, HD)
    ctx_values = ctx_v.reshape(N_CTX, BLK, KVH, HD)
    positions = jnp.arange(BLK)
    causal = positions[None, :] <= positions[:, None]

    def context_block(inputs):
        queries, key_rows, value_rows, block_index = inputs
        both_keys = jnp.concatenate([ctx_keys[0], key_rows], axis=0)
        both_values = jnp.concatenate([ctx_values[0], value_rows], axis=0)
        visible = jnp.concatenate([jnp.broadcast_to(block_index > 0, (BLK, BLK)), causal], axis=1)
        best_score, weight_sum, weighted = partials(queries, both_keys, both_values, visible)
        result = weighted / jnp.transpose(weight_sum, (2, 0, 1))[..., None]
        return result.astype(jnp.bfloat16).reshape(BLK, HQ * HD)

    context_out = lax.map(context_block, (ctx_queries, ctx_keys, ctx_values, jnp.arange(N_CTX)))
    context_out = context_out.reshape(N_CTX * BLK, HQ * HD)

    tail_queries = tail_q.reshape(TAIL, KVH, groups, HD)
    tail_keys = tail_k.reshape(N_CTX, tail_block, KVH, HD)
    tail_values = tail_v.reshape(N_CTX, tail_block, KVH, HD)
    query_pos = jnp.arange(TAIL)

    def tail_block_partials(inputs):
        key_rows, value_rows, extra_keys, extra_values, block_index = inputs
        key_pos = block_index * tail_block + jnp.arange(tail_block)
        visible = jnp.concatenate([jnp.ones((TAIL, BLK), jnp.bool_), key_pos[None, :] <= query_pos[:, None]], axis=1)
        return partials(tail_queries, jnp.concatenate([key_rows, extra_keys], axis=0), jnp.concatenate([value_rows, extra_values], axis=0), visible)

    all_best, all_sums, all_weighted = lax.map(tail_block_partials, (ctx_keys, ctx_values, tail_keys, tail_values, jnp.arange(N_CTX)))
    tail_top = jnp.max(all_best, axis=0)

    def add_block(state, inputs):
        numerator, denominator = state
        best_score, weight_sum, weighted = inputs
        factor = jnp.exp(best_score - tail_top)
        num_term = weighted * jnp.transpose(factor, (2, 0, 1))[..., None]
        den_term = weight_sum * factor
        return (numerator + num_term, denominator + den_term), None

    initial = (jnp.zeros((TAIL, KVH, groups, HD), jnp.float32), jnp.zeros((KVH, groups, TAIL), jnp.float32))
    final, unused = lax.scan(add_block, initial, (all_best, all_sums, all_weighted))
    numerator, denominator = final
    tail_attn = (numerator / jnp.transpose(denominator, (2, 0, 1))[..., None]).astype(jnp.bfloat16).reshape(TAIL, HQ * HD)
    tail_proj = jnp.dot(tail_attn, out_weight, preferred_element_type=jnp.float32)
    return context_out, tail_attn, tail_proj
```

```python
import functools

import jax
import jax.numpy as jnp
from jax import lax
from jax.experimental import pallas as pl
from jax.experimental.pallas import tpu as pltpu
from jax.sharding import PartitionSpec as P

HD = 128
HEADS = 8
BLK = 1024
ROWS = 16
GROUP = 128
XS, ZS, YS = 4, 8, 4
TILE = 256
PAD = 128
KEYS = 2 * BLK + PAD
LOG2E = 1.4426950408889634
C = LOG2E * HD ** (-0.5)
LOW = -1e30
TAIL_AT = 6
MERGE_AT = 5
NT = (((1,), (1,)), ((), ()))
MESH = pl.DeviceIdType.MESH
F32, BF16 = jnp.float32, jnp.bfloat16


def local_wait(ref, sem):
    pltpu.make_async_copy(ref, ref, sem).wait()


def weighted(scores, values):
    best = jnp.max(scores, axis=1, keepdims=True)
    weights = jnp.exp2((scores - best) * C).astype(BF16)
    return best, jnp.dot(weights, values, preferred_element_type=F32)


def kernel(
    q_hbm, k_hbm, v_hbm, tq_hbm, tk_hbm, tv_hbm, w_hbm,
    out_hbm, attn_hbm, proj_hbm,
    q, keys, vals, anchor, anchor_vals, acc, best_own, out,
    tail_q, bias, part, lse, got, got_lse, merged, weight, proj, pieces, result,
    load_sem, out_sem, q_send, q_recv, kv_send, kv_recv, a_send, a_recv,
    p_send, p_recv, m_send, m_recv, w_send, w_recv, r_send, r_recv,
):
    c, t = lax.axis_index("ctx"), lax.axis_index("tp")
    x, z, y, core = c // ZS, c % ZS, t // 2, t % 2
    pair = x + 1 - 2 * (x % 2)
    cross = XS - 1 - x
    far = (x + 2) % XS

    def at(dx, dz):
        return (dx * ZS + dz, t)

    def z_peer(i):
        return (z + i) % ZS

    def send(src, dst, s_sem, r_sem, device):
        pltpu.make_async_remote_copy(
            src_ref=src, dst_ref=dst, send_sem=s_sem, recv_sem=r_sem, device_id=device, device_id_type=MESH
        ).start()

    def rows16(i):
        return pl.ds(pl.multiple_of(i * ROWS, ROWS), ROWS)

    loads = [
        (k_hbm, keys.at[pl.ds(0, BLK)]),
        (v_hbm, vals.at[pl.ds(0, BLK), pl.ds(0, HD)]),
        (tk_hbm, keys.at[pl.ds(2 * BLK, ROWS)]),
        (tv_hbm, vals.at[pl.ds(2 * BLK, ROWS), pl.ds(0, HD)]),
        (q_hbm, q),
        (tq_hbm, tail_q.at[0, rows16(z)]),
        (w_hbm, weight.at[0]),
    ]
    keys[2 * BLK :, :] = jnp.zeros((PAD, HD), BF16)
    vals[2 * BLK :, :HD] = jnp.zeros((PAD, HD), BF16)
    copies = [pltpu.make_async_copy(a, b, load_sem.at[i]) for i, (a, b) in enumerate(loads)]
    for copy in copies:
        copy.start()

    barrier = pltpu.get_barrier_semaphore()

    def hello(device):
        pl.semaphore_signal(barrier, inc=1, device_id=device, device_id_type=MESH)

    for i in range(1, ZS):
        hello(at(x, z_peer(i)))
    for i in range(ZS):
        hello(at(cross, z_peer(i)))
    hello(at(pair, z))
    hello(at(far, z))
    own_in = jnp.logical_or(y == x, y == cross)
    source_x = jnp.where(own_in, x, pair)
    for sy in range(YS):
        for sc in range(2):
            mine = jnp.logical_and(own_in, t == 2 * sy + sc)

            @pl.when(jnp.logical_not(mine))
            def _():
                hello((source_x * ZS + z, 2 * sy + sc))

    vals[:, HD:] = jnp.ones((KEYS, HD), BF16)
    anchor_vals[:, HD:] = jnp.ones((BLK, HD), BF16)
    column = lax.broadcasted_iota(jnp.int32, (GROUP, PAD), 1)
    row = lax.broadcasted_iota(jnp.int32, (GROUP, PAD), 0)
    key_x = jnp.where(column < ROWS, x, pair)
    key_pos = key_x * GROUP + z * ROWS + column % ROWS
    for g, gx in ((0, x), (1, cross)):
        seen = jnp.logical_and(column < 2 * ROWS, key_pos <= gx * GROUP + row)
        bias[g] = jnp.where(seen, 0.0, LOW).astype(F32)
    lse[...] = jnp.zeros_like(lse)
    pl.semaphore_wait(barrier, 17 + jnp.where(own_in, 7, 8))

    def push_rows(src, dst, s_sem, r_sem):
        for i in range(ZS):
            send(src(1, z_peer(i)), dst(1), s_sem.at[1], r_sem.at[1], at(cross, z_peer(i)))
        for i in range(1, ZS):
            send(src(0, z_peer(i)), dst(0), s_sem.at[0], r_sem.at[0], at(x, z_peer(i)))

    push_rows(lambda g, i: tq_hbm, lambda g: tail_q.at[g, rows16(z)], q_send, q_recv)
    pair_device = at(pair, z)
    kv = [
        (k_hbm, keys.at[pl.ds(BLK, BLK)]),
        (v_hbm, vals.at[pl.ds(BLK, BLK), pl.ds(0, HD)]),
        (tk_hbm, keys.at[pl.ds(2 * BLK + ROWS, ROWS)]),
        (tv_hbm, vals.at[pl.ds(2 * BLK + ROWS, ROWS), pl.ds(0, HD)]),
    ]
    for i, (a, b) in enumerate(kv):
        send(a, b, kv_send.at[i], kv_recv.at[i], pair_device)

    half = BLK // 2
    piece = half // ZS
    sources = [k_hbm.at[pl.ds(0, half)], k_hbm.at[pl.ds(half, half)], v_hbm.at[pl.ds(0, half)], v_hbm.at[pl.ds(half, half)]]

    def quarter(i):
        return anchor.at[pl.ds(pl.multiple_of(i * half, half), half)]

    def piece_of(i, j):
        return anchor.at[pl.ds(pl.multiple_of(i * half + j * piece, piece), piece)]

    @pl.when(c == 0)
    def _():
        for i in range(1, XS):
            send(sources[i], quarter(i), a_send.at[i - 1], a_recv.at[0], at(i, 0))
        pltpu.make_async_copy(sources[0], quarter(0), load_sem.at[7]).start()

    def anchor_step_2():
        @pl.when(z == 0)
        def _():
            @pl.when(x > 0)
            def _():
                local_wait(quarter(x), a_recv.at[0])

            @pl.when(x == 0)
            def _():
                local_wait(quarter(0), load_sem.at[7])

            for i in range(1, ZS):
                send(piece_of(x, i), piece_of(x, i), a_send.at[3], a_recv.at[1], at(x, i))
            for i in range(1, ZS):
                send(piece_of(x, 0), piece_of(x, 0), a_send.at[4], a_recv.at[2], at(x, i))

    def anchor_step_3():
        @pl.when(z > 0)
        def _():
            local_wait(piece_of(x, z), a_recv.at[1])
            for i in range(1, ZS):
                @pl.when(z_peer(i) != 0)
                def _():
                    send(piece_of(x, z), piece_of(x, z), a_send.at[4], a_recv.at[2], at(x, z_peer(i)))

    def anchor_step_4():
        @pl.when(z > 0)
        def _():
            local_wait(anchor.at[pl.ds(0, 7 * piece)], a_recv.at[2])

        for i, dx in enumerate((pair, cross, far)):
            send(quarter(x), quarter(x), a_send.at[5], a_recv.at[3], at(dx, z))

    def anchor_step_5():
        local_wait(anchor.at[pl.ds(0, 3 * half)], a_recv.at[3])
        anchor_vals[:, :HD] = anchor[BLK:, :]

    def columns_of(h):
        return pl.ds(pl.multiple_of(h * HD, HD), HD)

    def tail_pair(g, j):
        first, second = columns_of(2 * j), columns_of(2 * j + 1)
        queries = jnp.concatenate([tail_q[g, :, first], tail_q[g, :, second]], axis=0)
        scores = lax.dot_general(queries, keys[...], NT, preferred_element_type=F32)
        seen = bias[g]
        last = scores[:, 2 * BLK :] + jnp.concatenate([seen, seen], axis=0)
        best, o = weighted(jnp.concatenate([scores[:, : 2 * BLK], last], axis=1), vals[...])
        total = o[:, HD:]
        normal = (o[:, :HD] / total).astype(BF16)
        part[g, :, first] = normal[:GROUP]
        part[g, :, second] = normal[GROUP:]
        level = best * C + jnp.log(total) * LOG2E
        lane = lax.broadcasted_iota(jnp.int32, (GROUP, HD), 1)
        now = jnp.where(lane == 2 * j, level[:GROUP], lse[g])
        lse[g] = jnp.where(lane == 2 * j + 1, level[GROUP:], now)

    def tail():
        local_wait(tail_q.at[1], q_recv.at[1])
        local_wait(tail_q.at[0, pl.ds(0, GROUP - ROWS)], q_recv.at[0])
        copies[5].wait()
        copies[2].wait()
        copies[3].wait()
        for i, (a, b) in enumerate(kv):
            local_wait(b, kv_recv.at[i])
        send(w_hbm, weight.at[1], w_send, w_recv, pair_device)

        def group_1(j, carry):
            tail_pair(1, j)
            return carry

        def group_0(j, carry):
            tail_pair(0, j)
            return carry

        lax.fori_loop(0, HEADS // 2, group_1, 0)
        for i in range(ZS):
            there = z_peer(i)
            send(part.at[1, rows16(there)], got.at[1, rows16(z)], p_send.at[1], p_recv.at[1], at(cross, there))
            send(lse.at[1, rows16(there)], got_lse.at[1, rows16(z)], p_send.at[3], p_recv.at[3], at(cross, there))
        lax.fori_loop(0, HEADS // 2, group_0, 0)
        for i in range(1, ZS):
            there = z_peer(i)
            send(part.at[0, rows16(there)], got.at[0, rows16(z)], p_send.at[0], p_recv.at[0], at(x, there))
            send(lse.at[0, rows16(there)], got_lse.at[0, rows16(z)], p_send.at[2], p_recv.at[2], at(x, there))
        got[0, rows16(z), :] = part[0, rows16(z), :]
        got_lse[0, rows16(z), :] = lse[0, rows16(z), :]

    short = pl.ds(0, GROUP - ROWS)

    def merge():
        local_wait(got.at[1], p_recv.at[1])
        local_wait(got_lse.at[1], p_recv.at[3])
        local_wait(got.at[0, short], p_recv.at[0])
        local_wait(got_lse.at[0, short], p_recv.at[2])
        levels = got_lse[...].reshape(2 * ZS, ROWS, HD)
        factors = jnp.exp2(levels - jnp.max(levels, axis=0, keepdims=True))
        factors = factors / jnp.sum(factors, axis=0, keepdims=True)
        for h in range(HEADS):
            cols = slice(h * HD, (h + 1) * HD)
            total = jnp.zeros((ROWS, HD), F32)
            for s in range(2 * ZS):
                g, i = s // ZS, s % ZS
                term = got[g, i * ROWS : (i + 1) * ROWS, cols].astype(F32)
                total = total + term * factors[s, :, h : h + 1]
            merged[0, rows16(z), cols] = total.astype(BF16)
        mine = merged.at[0, rows16(z)]
        push_rows(lambda g, i: mine, lambda g: merged.at[g, rows16(z)], m_send, m_recv)
        pltpu.make_async_copy(mine, attn_hbm, out_sem.at[8]).start()

    def own_head(h, carry):
        pl.when(h == 2)(anchor_step_2)
        pl.when(h == 4)(anchor_step_3)

        @pl.when(h == TAIL_AT)
        def _():
            anchor_step_4()
            tail()

        cols = columns_of(h)
        at_row = lax.broadcasted_iota(jnp.int32, (TILE, TILE), 0)
        at_col = lax.broadcasted_iota(jnp.int32, (TILE, TILE), 1)
        for i in range(BLK // TILE):
            rows, n = slice(i * TILE, (i + 1) * TILE), (i + 1) * TILE
            scores = lax.dot_general(q[rows, cols], keys[:n, :], NT, preferred_element_type=F32)
            last = jnp.where(at_col <= at_row, scores[:, n - TILE :], LOW)
            scores = jnp.concatenate([scores[:, : n - TILE], last], axis=1) if i else last
            best, o = weighted(scores, vals[:n, :])
            acc[h, rows, :] = o
            best_own[h, rows, :] = jnp.broadcast_to(best, (TILE, HD))
        return carry

    def anchor_head(h, carry):
        pl.when(h == MERGE_AT)(merge)
        cols = columns_of(h)
        for i in range(BLK // TILE):
            rows = slice(i * TILE, (i + 1) * TILE)
            scores = lax.dot_general(q[rows, cols], anchor[:BLK, :], NT, preferred_element_type=F32)
            best, o = weighted(scores, anchor_vals[...])
            best = jnp.where(c == 0, LOW, jnp.broadcast_to(best, (TILE, HD)))
            before = best_own[h, rows, :]
            top = jnp.maximum(before, best)
            f_own, f_anchor = jnp.exp2((before - top) * C), jnp.exp2((best - top) * C)
            own = acc[h, rows, :]
            num = own[:, :HD] * f_own + o[:, :HD] * f_anchor
            den = own[:, HD:] * f_own + o[:, HD:] * f_anchor
            out[rows, cols] = (num / den).astype(BF16)
        pltpu.make_async_copy(out.at[:, cols], out_hbm.at[:, cols], out_sem.at[h]).start()
        return carry

    copies[0].wait()
    copies[1].wait()
    copies[4].wait()
    lax.fori_loop(0, HEADS, own_head, 0)
    anchor_step_5()
    lax.fori_loop(0, HEADS, anchor_head, 0)

    copies[6].wait()
    local_wait(weight.at[1], w_recv)
    local_wait(merged.at[1], m_recv.at[1])
    local_wait(merged.at[0, short], m_recv.at[0])
    rows_all = merged[...].reshape(2 * GROUP, HEADS * HD)
    for j in range(2):
        proj[j] = jnp.dot(rows_all, weight[j], preferred_element_type=F32).astype(BF16)
    for g, gy in ((0, x), (1, cross)):
        for k in range(2):
            for j, jx in ((0, x), (1, pair)):
                src = proj.at[j, pl.ds(g * GROUP + k * 64, 64)]
                to = 2 * gy + k
                if j == 0:
                    @pl.when(to == t)
                    def _():
                        pieces[t] = src[...]

                    @pl.when(to != t)
                    def _():
                        send(src, pieces.at[t], r_send, r_recv, (c, to))
                else:
                    send(src, pieces.at[t], r_send, r_recv, (jx * ZS + z, to))

    @pl.when(own_in)
    def _():
        local_wait(pieces.at[pl.ds(0, 7)], r_recv)

    @pl.when(jnp.logical_not(own_in))
    def _():
        local_wait(pieces, r_recv)

    total = pieces[0].astype(F32)
    for i in range(1, 8):
        total = total + pieces[i].astype(F32)
    result[...] = total
    last = pltpu.make_async_copy(result, proj_hbm, out_sem.at[9])
    last.start()

    for h in range(HEADS):
        cols = pl.ds(h * HD, HD)
        pltpu.make_async_copy(out.at[:, cols], out_hbm.at[:, cols], out_sem.at[h]).wait()
    pltpu.make_async_copy(merged.at[0, rows16(z)], attn_hbm, out_sem.at[8]).wait()
    for ref, sem in ((tail_q, q_send), (part, p_send), (merged, m_send)):
        local_wait(ref.at[1], sem.at[1])
        local_wait(ref.at[0, short], sem.at[0])
    local_wait(lse.at[1], p_send.at[3])
    local_wait(lse.at[0, short], p_send.at[2])
    for i, (a, b) in enumerate(kv):
        local_wait(b, kv_send.at[i])
    local_wait(weight.at[1], w_send)

    @pl.when(c == 0)
    def _():
        for i in range(1, XS):
            local_wait(quarter(i), a_send.at[i - 1])

    @pl.when(z == 0)
    def _():
        local_wait(anchor.at[pl.ds(0, 7 * piece)], a_send.at[3])
        local_wait(anchor.at[pl.ds(0, 7 * piece)], a_send.at[4])

    @pl.when(z > 0)
    def _():
        local_wait(anchor.at[pl.ds(0, 6 * piece)], a_send.at[4])

    local_wait(anchor.at[pl.ds(0, 3 * half)], a_send.at[5])

    @pl.when(own_in)
    def _():
        local_wait(pieces.at[pl.ds(0, 7)], r_send)

    @pl.when(jnp.logical_not(own_in))
    def _():
        local_wait(pieces, r_send)

    last.wait()


def on_device(*args):
    width = HEADS * HD
    dma = pltpu.SemaphoreType.DMA
    return pl.pallas_call(
        kernel,
        out_shape=(
            jax.ShapeDtypeStruct((BLK, width), BF16),
            jax.ShapeDtypeStruct((ROWS, width), BF16),
            jax.ShapeDtypeStruct((64, 256), F32),
        ),
        in_specs=[pl.BlockSpec(memory_space=pl.ANY)] * 7,
        out_specs=[pl.BlockSpec(memory_space=pl.ANY)] * 3,
        scratch_shapes=[
            pltpu.VMEM((BLK, width), BF16),
            pltpu.VMEM((KEYS, HD), BF16),
            pltpu.VMEM((KEYS, 2 * HD), BF16),
            pltpu.VMEM((2 * BLK, HD), BF16),
            pltpu.VMEM((BLK, 2 * HD), BF16),
            pltpu.VMEM((HEADS, BLK, 2 * HD), F32),
            pltpu.VMEM((HEADS, BLK, HD), F32),
            pltpu.VMEM((BLK, width), BF16),
            pltpu.VMEM((2, GROUP, width), BF16),
            pltpu.VMEM((2, GROUP, PAD), F32),
            pltpu.VMEM((2, GROUP, width), BF16),
            pltpu.VMEM((2, GROUP, HD), F32),
            pltpu.VMEM((2, GROUP, width), BF16),
            pltpu.VMEM((2, GROUP, HD), F32),
            pltpu.VMEM((2, GROUP, width), BF16),
            pltpu.VMEM((2, width, 256), BF16),
            pltpu.VMEM((2, 2 * GROUP, 256), BF16),
            pltpu.VMEM((8, 64, 256), BF16),
            pltpu.VMEM((64, 256), F32),
            dma((8,)),
            dma((10,)),
            dma((2,)), dma((2,)),
            dma((4,)), dma((4,)),
            dma((6,)), dma((4,)),
            dma((4,)), dma((4,)),
            dma((2,)), dma((2,)),
            dma, dma,
            dma, dma,
        ],
        compiler_params=pltpu.CompilerParams(
            collective_id=0, has_side_effects=True, vmem_limit_bytes=56 * 2**20
        ),
    )(*args)


def solution(mesh):
    placed = (P("ctx", "tp"),) * 6 + (P("tp", "ctx"),)
    return jax.shard_map(
        on_device,
        mesh=mesh,
        in_specs=placed,
        out_specs=(P("ctx", "tp"), P("ctx", "tp"), P("tp", "ctx")),
        check_vma=False,
    )
```

```python
import functools

import jax
import jax.numpy as jnp
from jax import lax
from jax.experimental import pallas as pl
from jax.experimental.pallas import tpu as pltpu
from jax.sharding import PartitionSpec as P

HD = 128
HEADS = 8
BLK = 1024
ROWS = 16
GROUP = 128
XS, ZS, YS = 4, 8, 4
TILE = 256
PAD = 128
KEYS = BLK + PAD
HALF = HEADS // 2 * HD
WIDE = HALF + HD
LOG2E = 1.4426950408889634
C = LOG2E * HD ** (-0.5)
LOW = -1e30
CHUNKS = 8
GREET_AT, FIRST_AT, TAIL_AT, MERGE_A_AT = 0, 4, 5, 7
MERGE_B_AT, PROJECT_AT = 1, 5
NT = (((1,), (1,)), ((), ()))
MESH = pl.DeviceIdType.MESH
F32, BF16 = jnp.float32, jnp.bfloat16


def local_wait(ref, sem):
    pltpu.make_async_copy(ref, ref, sem).wait()


def weighted(scores, values):
    best = jnp.max(scores, axis=1, keepdims=True)
    weights = jnp.exp2((scores - best) * C).astype(BF16)
    return best, jnp.dot(weights, values, preferred_element_type=F32)


def copy_out(*refs):
    sources, results, buffers, sems = refs[:3], refs[3:6], refs[6:9], refs[9]
    step = BLK // CHUNKS
    parts = [(i, pl.ds(0, results[i].shape[0])) for i in (1, 2)]
    parts = [(0, pl.ds(i * step, step)) for i in range(CHUNKS)] + parts
    loads = [pltpu.make_async_copy(sources[i].at[s], buffers[i].at[s], sems.at[0, n]) for n, (i, s) in enumerate(parts)]
    stores = [pltpu.make_async_copy(buffers[i].at[s], results[i].at[s], sems.at[1, n]) for n, (i, s) in enumerate(parts)]
    for copy in loads:
        copy.start()
    for load, store in zip(loads, stores):
        load.wait()
        store.start()
    for copy in stores:
        copy.wait()


def kernel(
    q_hbm, k_hbm, v_hbm, tq_hbm, tk_hbm, tv_hbm, w_hbm,
    out_hbm, attn_hbm, proj_hbm,
    q, keys, vals, anchor, anchor_vals, acc, best_own, out,
    tail_q, bias, tail_acc, tail_best, part, got, merged, weight, proj, pieces, result,
    load_sem, out_sem, q_send, q_recv, kv_send, kv_recv, a_send, a_recv,
    p_send, p_recv, m_send, m_recv, w_send, w_recv, r_send, r_recv,
):
    c, t = lax.axis_index("ctx"), lax.axis_index("tp")
    x, z, y = c // ZS, c % ZS, t // 2
    pair = x + 1 - 2 * (x % 2)
    cross = XS - 1 - x
    far = (x + 2) % XS

    def at(dx, dz):
        return (dx * ZS + dz, t)

    def z_peer(i):
        return (z + i) % ZS

    def send(src, dst, s_sem, r_sem, device):
        pltpu.make_async_remote_copy(
            src_ref=src, dst_ref=dst, send_sem=s_sem, recv_sem=r_sem, device_id=device, device_id_type=MESH
        ).start()

    def rows16(i):
        return pl.ds(pl.multiple_of(i * ROWS, ROWS), ROWS)

    loads = [
        (k_hbm, keys.at[0, pl.ds(0, BLK)]),
        (v_hbm, vals.at[0, pl.ds(0, BLK), pl.ds(0, HD)]),
        (q_hbm, q),
        (tk_hbm, keys.at[0, pl.ds(BLK, ROWS)]),
        (tv_hbm, vals.at[0, pl.ds(BLK, ROWS), pl.ds(0, HD)]),
        (tq_hbm, tail_q.at[0, rows16(z)]),
        (w_hbm, weight.at[0]),
    ]
    for b in range(2):
        keys[b, BLK:, :] = jnp.zeros((PAD, HD), BF16)
        vals[b, BLK:, :HD] = jnp.zeros((PAD, HD), BF16)
    copies = [pltpu.make_async_copy(a, b, load_sem.at[i]) for i, (a, b) in enumerate(loads)]
    for copy in copies:
        copy.start()

    barrier = pltpu.get_barrier_semaphore()

    def hello(device):
        pl.semaphore_signal(barrier, inc=1, device_id=device, device_id_type=MESH)

    for i in range(1, ZS):
        hello(at(x, z_peer(i)))
    for i in range(ZS):
        hello(at(cross, z_peer(i)))
    hello(at(pair, z))
    hello(at(far, z))
    own_in = jnp.logical_or(y == x, y == cross)
    source_x = jnp.where(own_in, x, pair)
    for s in range(8):
        @pl.when(jnp.logical_not(jnp.logical_and(own_in, t == s)))
        def _():
            hello((source_x * ZS + z, s))

    @pl.when(jnp.logical_and(z > 0, jnp.logical_or(x == 1, x == 2)))
    def _():
        hello((0, t))

    for b in range(2):
        vals[b, :, HD:] = jnp.ones((KEYS, HD), BF16)
    anchor_vals[:, HD:] = jnp.ones((BLK, HD), BF16)
    column = lax.broadcasted_iota(jnp.int32, (GROUP, PAD), 1)
    row = lax.broadcasted_iota(jnp.int32, (GROUP, PAD), 0)
    for g, gx in ((0, x), (1, cross)):
        for b, bx in ((0, x), (1, pair)):
            key_pos = bx * GROUP + z * ROWS + column
            seen = jnp.logical_and(column < ROWS, key_pos <= gx * GROUP + row)
            bias[g, b] = jnp.where(seen, 0.0, LOW).astype(F32)

    def push_own(src, dst, s_sem, r_sem):
        for i in range(1, ZS):
            there = z_peer(i)
            send(src(there), dst, s_sem, r_sem, at(x, there))

    def push_cross(src, dst, s_sem, r_sem):
        for i in range(ZS):
            there = z_peer(i)
            send(src(there), dst, s_sem, r_sem, at(cross, there))

    pair_device = at(pair, z)
    kv = [
        (k_hbm, keys.at[1, pl.ds(0, BLK)]),
        (v_hbm, vals.at[1, pl.ds(0, BLK), pl.ds(0, HD)]),
        (tk_hbm, keys.at[1, pl.ds(BLK, ROWS)]),
        (tv_hbm, vals.at[1, pl.ds(BLK, ROWS), pl.ds(0, HD)]),
    ]

    piece = 2 * BLK // (XS * ZS)
    in_keys = BLK // piece
    quarter_rows = ZS * piece

    def piece_of(i):
        return anchor.at[pl.ds(pl.multiple_of(i * piece, piece), piece)]

    def quarter(i):
        return anchor.at[pl.ds(pl.multiple_of(i * quarter_rows, quarter_rows), quarter_rows)]

    def greet():
        pl.semaphore_wait(barrier, 17 + jnp.where(own_in, 7, 8) + jnp.where(c == 0, 14, 0))

        @pl.when(c == 0)
        def _():
            def from_keys(i, carry):
                src = k_hbm.at[pl.ds(pl.multiple_of(i * piece, piece), piece)]
                send(src, piece_of(i), a_send.at[0], a_recv.at[0], (i, t))
                return carry

            def from_values(i, carry):
                src = v_hbm.at[pl.ds(pl.multiple_of((i - in_keys) * piece, piece), piece)]
                send(src, piece_of(i), a_send.at[0], a_recv.at[0], (i, t))
                return carry

            lax.fori_loop(1, in_keys, from_keys, 0)
            lax.fori_loop(in_keys, XS * ZS, from_values, 0)
            pltpu.make_async_copy(k_hbm.at[pl.ds(0, piece)], piece_of(0), load_sem.at[7]).start()

        push_own(lambda there: tq_hbm, tail_q.at[0, rows16(z)], q_send.at[0], q_recv.at[0])
        for i, (a, b) in enumerate(kv):
            send(a, b, kv_send.at[i], kv_recv.at[i], pair_device)

    def anchor_along_z():
        @pl.when(c > 0)
        def _():
            local_wait(piece_of(c), a_recv.at[0])

        @pl.when(c == 0)
        def _():
            local_wait(piece_of(0), load_sem.at[7])

        for i in range(1, ZS):
            send(piece_of(c), piece_of(c), a_send.at[1], a_recv.at[1], at(x, z_peer(i)))

    def anchor_along_x():
        local_wait(anchor.at[pl.ds(0, (ZS - 1) * piece)], a_recv.at[1])
        for dx in (pair, cross, far):
            send(quarter(x), quarter(x), a_send.at[2], a_recv.at[2], at(dx, z))

    def anchor_ready():
        local_wait(anchor.at[pl.ds(0, 3 * quarter_rows)], a_recv.at[2])
        anchor_vals[:, :HD] = anchor[BLK:, :]

    def columns_of(h):
        return pl.ds(pl.multiple_of(h * HD, HD), HD)

    short = pl.ds(0, GROUP - ROWS)

    def tail_block(b, g, j):
        first, second = columns_of(2 * j), columns_of(2 * j + 1)
        queries = jnp.concatenate([tail_q[g, :, first], tail_q[g, :, second]], axis=0)
        scores = lax.dot_general(queries, keys[b], NT, preferred_element_type=F32)
        seen = bias[g, b]
        last = scores[:, BLK:] + jnp.concatenate([seen, seen], axis=0)
        best, o = weighted(jnp.concatenate([scores[:, :BLK], last], axis=1), vals[b])
        return jnp.broadcast_to(best, (2 * GROUP, HD)), o

    def half_of(a):
        return pl.ds(pl.multiple_of(a * WIDE, HD), WIDE)

    def tail_finish(g, a, blocks):
        lane = lax.broadcasted_iota(jnp.int32, (GROUP, HD), 1)
        held = jnp.zeros((GROUP, HD), F32)
        for i, ((best_1, o_1), (best_2, o_2)) in enumerate(blocks):
            top = jnp.maximum(best_1, best_2)
            f_1, f_2 = jnp.exp2((best_1 - top) * C), jnp.exp2((best_2 - top) * C)
            num = o_1[:, :HD] * f_1 + o_2[:, :HD] * f_2
            den = o_1[:, HD:] * f_1 + o_2[:, HD:] * f_2
            normal = (num / den).astype(BF16)
            level = top * C + jnp.log(den) * LOG2E
            high = level.astype(BF16).astype(F32)
            middle = (level - high).astype(BF16).astype(F32)
            low = level - high - middle
            for k in range(2):
                h = 2 * i + k
                rows = slice(k * GROUP, (k + 1) * GROUP)
                part[g, :, pl.ds(pl.multiple_of(a * WIDE + h * HD, HD), HD)] = normal[rows]
                held = jnp.where(lane == h, high[rows], held)
                held = jnp.where(lane == h + 8, middle[rows], held)
                held = jnp.where(lane == h + 16, low[rows], held)
        part[g, :, pl.ds(pl.multiple_of(a * WIDE + HALF, HD), HD)] = held.astype(BF16)

    def tail_first():
        local_wait(tail_q.at[0, short], q_recv.at[0])
        for i in (3, 4, 5):
            copies[i].wait()
        send(tail_q.at[0], tail_q.at[1], q_send.at[1], q_recv.at[1], at(cross, z))

        def own_block(a, carry):
            for j in (2 * a, 2 * a + 1):
                best, o = tail_block(0, 0, j)
                tail_acc[j] = o
                tail_best[j] = best
            return carry

        lax.fori_loop(0, 2, own_block, 0)
        anchor_along_z()

    def tail():
        for i, (a, b) in enumerate(kv):
            local_wait(b, kv_recv.at[i])

        def group_0(a, carry):
            blocks = []
            for j in (2 * a, 2 * a + 1):
                other = tail_block(1, 0, j)
                blocks.append(((tail_best[j], tail_acc[j]), other))
            tail_finish(0, a, blocks)
            return carry

        lax.fori_loop(0, 2, group_0, 0)
        push_own(lambda there: part.at[0, rows16(there)], got.at[0, rows16(z)], p_send.at[0], p_recv.at[0])
        got[0, rows16(z), :] = part[0, rows16(z), :]
        local_wait(tail_q.at[1], q_recv.at[1])

        def group_1(a, carry):
            tail_finish(1, a, [(tail_block(0, 1, j), tail_block(1, 1, j)) for j in (2 * a, 2 * a + 1)])
            push_cross(
                lambda there: part.at[1, rows16(there), half_of(a)],
                got.at[1, rows16(z), half_of(a)],
                p_send.at[1 + a],
                p_recv.at[1 + a],
            )
            return carry

        lax.fori_loop(0, 2, group_1, 0)
        anchor_along_x()
        send(w_hbm, weight.at[1], w_send, w_recv, pair_device)

    def merge(a):
        if a == 0:
            local_wait(got.at[0, short], p_recv.at[0])
        local_wait(got.at[1, :, half_of(a)], p_recv.at[1 + a])
        levels = got[:, :, a * WIDE + HALF : (a + 1) * WIDE].astype(F32).reshape(2 * GROUP, HD)
        levels = levels + pltpu.roll(levels, HD - 8, 1) + pltpu.roll(levels, HD - 16, 1)
        levels = levels.reshape(2 * ZS, ROWS, HD)
        factors = jnp.exp2(levels - jnp.max(levels, axis=0, keepdims=True))
        factors = factors / jnp.sum(factors, axis=0, keepdims=True)
        for h in range(HEADS // 2):
            total = jnp.zeros((ROWS, HD), F32)
            for s in range(2 * ZS):
                g, i = s // ZS, s % ZS
                term = got[g, i * ROWS : (i + 1) * ROWS, a * WIDE + h * HD : a * WIDE + (h + 1) * HD].astype(F32)
                total = total + term * factors[s, :, h : h + 1]
            merged[a, 0, rows16(z), h * HD : (h + 1) * HD] = total.astype(BF16)
        mine = merged.at[a, 0, rows16(z)]
        push_cross(lambda there: mine, merged.at[a, 1, rows16(z)], m_send.at[a, 1], m_recv.at[a, 1])
        push_own(lambda there: mine, merged.at[a, 0, rows16(z)], m_send.at[a, 0], m_recv.at[a, 0])
        pltpu.make_async_copy(mine, attn_hbm.at[:, pl.ds(a * HALF, HALF)], out_sem.at[8 + a]).start()

    def project():
        copies[6].wait()
        local_wait(weight.at[1], w_recv)
        for a in range(2):
            local_wait(merged.at[a, 0, short], m_recv.at[a, 0])
            local_wait(merged.at[a, 1], m_recv.at[a, 1])
        for j, jx in ((1, pair), (0, x)):
            projected = jnp.zeros((2 * GROUP, 256), F32)
            for a in range(2):
                rows = merged[a].reshape(2 * GROUP, HALF)
                projected += jnp.dot(rows, weight[j, a * HALF : (a + 1) * HALF, :], preferred_element_type=F32)
            proj[j] = projected.astype(BF16)
            for g, gy in ((0, x), (1, cross)):
                for k in range(2):
                    src = proj.at[j, pl.ds(g * GROUP + k * 64, 64)]
                    to = 2 * gy + k
                    if j == 0:
                        @pl.when(to == t)
                        def _():
                            pieces[t] = src[...]

                        @pl.when(to != t)
                        def _():
                            send(src, pieces.at[t], r_send, r_recv, (c, to))
                    else:
                        send(src, pieces.at[t], r_send, r_recv, (jx * ZS + z, to))

    def own_head(h, carry):
        pl.when(h == GREET_AT)(greet)
        pl.when(h == FIRST_AT)(tail_first)
        pl.when(h == TAIL_AT)(tail)
        pl.when(h == MERGE_A_AT)(functools.partial(merge, 0))
        cols = columns_of(h)
        at_row = lax.broadcasted_iota(jnp.int32, (TILE, TILE), 0)
        at_col = lax.broadcasted_iota(jnp.int32, (TILE, TILE), 1)
        for i in range(BLK // TILE):
            rows, n = slice(i * TILE, (i + 1) * TILE), (i + 1) * TILE
            scores = lax.dot_general(q[rows, cols], keys[0, :n, :], NT, preferred_element_type=F32)
            last = jnp.where(at_col <= at_row, scores[:, n - TILE :], LOW)
            scores = jnp.concatenate([scores[:, : n - TILE], last], axis=1) if i else last
            best, o = weighted(scores, vals[0, :n, :])
            acc[h, rows, :] = o
            best_own[h, rows, :] = jnp.broadcast_to(best, (TILE, HD))
        return carry

    def anchor_head(h, carry):
        pl.when(h == MERGE_B_AT)(functools.partial(merge, 1))
        pl.when(h == PROJECT_AT)(project)
        cols = columns_of(h)
        for i in range(BLK // TILE):
            rows = slice(i * TILE, (i + 1) * TILE)
            scores = lax.dot_general(q[rows, cols], anchor[:BLK, :], NT, preferred_element_type=F32)
            best, o = weighted(scores, anchor_vals[...])
            best = jnp.where(c == 0, LOW, jnp.broadcast_to(best, (TILE, HD)))
            before = best_own[h, rows, :]
            top = jnp.maximum(before, best)
            f_own, f_anchor = jnp.exp2((before - top) * C), jnp.exp2((best - top) * C)
            own = acc[h, rows, :]
            num = own[:, :HD] * f_own + o[:, :HD] * f_anchor
            den = own[:, HD:] * f_own + o[:, HD:] * f_anchor
            out[rows, cols] = (num / den).astype(BF16)
        pltpu.make_async_copy(out.at[:, cols], out_hbm.at[:, cols], out_sem.at[h]).start()
        return carry

    if GREET_AT < 0:
        greet()
    for i in range(3):
        copies[i].wait()
    lax.fori_loop(0, HEADS, own_head, 0)
    anchor_ready()
    lax.fori_loop(0, HEADS, anchor_head, 0)

    for h in range(HEADS):
        cols = pl.ds(h * HD, HD)
        pltpu.make_async_copy(out.at[:, cols], out_hbm.at[:, cols], out_sem.at[h]).wait()
    for a in range(2):
        pltpu.make_async_copy(merged.at[a, 0, rows16(z)], attn_hbm.at[:, pl.ds(a * HALF, HALF)], out_sem.at[8 + a]).wait()
        local_wait(merged.at[a, 0, short], m_send.at[a, 0])
        local_wait(merged.at[a, 1], m_send.at[a, 1])
        local_wait(part.at[1, :, half_of(a)], p_send.at[1 + a])
    local_wait(part.at[0, short], p_send.at[0])
    local_wait(tail_q.at[0, short], q_send.at[0])
    local_wait(tail_q.at[1], q_send.at[1])
    for i, (a, b) in enumerate(kv):
        local_wait(b, kv_send.at[i])
    local_wait(weight.at[1], w_send)

    @pl.when(c == 0)
    def _():
        local_wait(anchor.at[pl.ds(0, (XS * ZS - 1) * piece)], a_send.at[0])

    local_wait(anchor.at[pl.ds(0, (ZS - 1) * piece)], a_send.at[1])
    local_wait(anchor.at[pl.ds(0, 3 * quarter_rows)], a_send.at[2])

    for sem in (r_recv, r_send):
        @pl.when(own_in)
        def _():
            local_wait(pieces.at[pl.ds(0, 7)], sem)

        @pl.when(jnp.logical_not(own_in))
        def _():
            local_wait(pieces, sem)

    total = pieces[0].astype(F32)
    for i in range(1, 8):
        total = total + pieces[i].astype(F32)
    result[...] = total
    last = pltpu.make_async_copy(result, proj_hbm, out_sem.at[10])
    last.start()
    last.wait()


def on_device(*args):
    width = HEADS * HD
    dma = pltpu.SemaphoreType.DMA
    shapes = (
        jax.ShapeDtypeStruct((BLK, width), BF16),
        jax.ShapeDtypeStruct((ROWS, width), BF16),
        jax.ShapeDtypeStruct((64, 256), F32),
    )
    results = pl.pallas_call(
        kernel,
        out_shape=shapes,
        in_specs=[pl.BlockSpec(memory_space=pl.ANY)] * 7,
        out_specs=[pl.BlockSpec(memory_space=pl.ANY)] * 3,
        scratch_shapes=[
            pltpu.VMEM((BLK, width), BF16),
            pltpu.VMEM((2, KEYS, HD), BF16),
            pltpu.VMEM((2, KEYS, 2 * HD), BF16),
            pltpu.VMEM((2 * BLK, HD), BF16),
            pltpu.VMEM((BLK, 2 * HD), BF16),
            pltpu.VMEM((HEADS, BLK, 2 * HD), F32),
            pltpu.VMEM((HEADS, BLK, HD), F32),
            pltpu.VMEM((BLK, width), BF16),
            pltpu.VMEM((2, GROUP, width), BF16),
            pltpu.VMEM((2, 2, GROUP, PAD), F32),
            pltpu.VMEM((HEADS // 2, 2 * GROUP, 2 * HD), F32),
            pltpu.VMEM((HEADS // 2, 2 * GROUP, HD), F32),
            pltpu.VMEM((2, GROUP, 2 * WIDE), BF16),
            pltpu.VMEM((2, GROUP, 2 * WIDE), BF16),
            pltpu.VMEM((2, 2, GROUP, HALF), BF16),
            pltpu.VMEM((2, width, 256), BF16),
            pltpu.VMEM((2, 2 * GROUP, 256), BF16),
            pltpu.VMEM((8, 64, 256), BF16),
            pltpu.VMEM((64, 256), F32),
            dma((8,)),
            dma((11,)),
            dma((2,)), dma((2,)),
            dma((4,)), dma((4,)),
            dma((3,)), dma((3,)),
            dma((3,)), dma((3,)),
            dma((2, 2)), dma((2, 2)),
            dma, dma,
            dma, dma,
        ],
        compiler_params=pltpu.CompilerParams(
            collective_id=0, has_side_effects=True, vmem_limit_bytes=56 * 2**20
        ),
    )(*args)
    return pl.pallas_call(
        copy_out,
        out_shape=shapes,
        in_specs=[pl.BlockSpec(memory_space=pltpu.HBM)] * 3,
        out_specs=[pl.BlockSpec(memory_space=pltpu.HBM)] * 3,
        scratch_shapes=[pltpu.VMEM(s.shape, s.dtype) for s in shapes] + [dma((2, CHUNKS + 2))],
        compiler_params=pltpu.CompilerParams(vmem_limit_bytes=56 * 2**20),
    )(*results)


def solution(mesh):
    placed = (P("ctx", "tp"),) * 6 + (P("tp", "ctx"),)
    return jax.shard_map(
        on_device,
        mesh=mesh,
        in_specs=placed,
        out_specs=(P("ctx", "tp"), P("ctx", "tp"), P("tp", "ctx")),
        check_vma=False,
    )
```

```python
import functools

import jax
import jax.numpy as jnp
from jax import lax
from jax.experimental import pallas as pl
from jax.experimental.pallas import tpu as pltpu
from jax.sharding import PartitionSpec as P

HD = 128
HEADS = 8
BLK = 1024
ROWS = 16
GROUP = 128
XS, ZS, YS = 4, 8, 4
TILE = 256
PAD = 128
KEYS = BLK + PAD
HALF = HEADS // 2 * HD
WIDE = HALF + HD
LOG2E = 1.4426950408889634
C = LOG2E * HD ** (-0.5)
LOW = -1e30
CHUNKS = 8
GREET_AT, FIRST_AT, TAIL_AT, MERGE_A_AT = 0, 4, 5, 7
MERGE_B_AT, PROJECT_AT = 1, 5
NT = (((1,), (1,)), ((), ()))
MESH = pl.DeviceIdType.MESH
F32, BF16 = jnp.float32, jnp.bfloat16


def local_wait(ref, sem):
    pltpu.make_async_copy(ref, ref, sem).wait()


def weighted(scores, values):
    best = jnp.max(scores, axis=1, keepdims=True)
    weights = jnp.exp2((scores - best) * C).astype(BF16)
    return best, jnp.dot(weights, values, preferred_element_type=F32)


def copy_out(*refs):
    sources, results, buffers, sems = refs[:3], refs[3:6], refs[6:9], refs[9]
    step = BLK // CHUNKS
    parts = [(i, pl.ds(0, results[i].shape[0])) for i in (1, 2)]
    parts = [(0, pl.ds(i * step, step)) for i in range(CHUNKS)] + parts
    loads = [pltpu.make_async_copy(sources[i].at[s], buffers[i].at[s], sems.at[0, n]) for n, (i, s) in enumerate(parts)]
    stores = [pltpu.make_async_copy(buffers[i].at[s], results[i].at[s], sems.at[1, n]) for n, (i, s) in enumerate(parts)]
    for copy in loads:
        copy.start()
    for load, store in zip(loads, stores):
        load.wait()
        store.start()
    for copy in stores:
        copy.wait()


def kernel(
    q_hbm, k_hbm, v_hbm, tq_hbm, tk_hbm, tv_hbm, w_hbm,
    out_hbm, attn_hbm, proj_hbm,
    q, keys, vals, anchor, anchor_vals, acc, best_own, out,
    tail_q, bias, tail_acc, tail_best, part, got, merged, weight, proj, pieces, result,
    load_sem, out_sem, q_send, q_recv, kv_send, kv_recv, a_send, a_recv,
    p_send, p_recv, m_send, m_recv, w_send, w_recv, r_send, r_recv,
):
    c, t = lax.axis_index("ctx"), lax.axis_index("tp")
    x, z, y = c // ZS, c % ZS, t // 2
    pair = x + 1 - 2 * (x % 2)
    cross = XS - 1 - x
    far = (x + 2) % XS

    def at(dx, dz):
        return (dx * ZS + dz, t)

    def z_peer(i):
        return (z + i) % ZS

    def send(src, dst, s_sem, r_sem, device):
        pltpu.make_async_remote_copy(
            src_ref=src, dst_ref=dst, send_sem=s_sem, recv_sem=r_sem, device_id=device, device_id_type=MESH
        ).start()

    def rows16(i):
        return pl.ds(pl.multiple_of(i * ROWS, ROWS), ROWS)

    loads = [
        (k_hbm, keys.at[0, pl.ds(0, BLK)]),
        (v_hbm, vals.at[0, pl.ds(0, BLK), pl.ds(0, HD)]),
        (q_hbm, q),
        (tk_hbm, keys.at[0, pl.ds(BLK, ROWS)]),
        (tv_hbm, vals.at[0, pl.ds(BLK, ROWS), pl.ds(0, HD)]),
        (tq_hbm, tail_q.at[0, rows16(z)]),
        (w_hbm, weight.at[0]),
    ]
    for b in range(2):
        keys[b, BLK:, :] = jnp.zeros((PAD, HD), BF16)
        vals[b, BLK:, :HD] = jnp.zeros((PAD, HD), BF16)
    copies = [pltpu.make_async_copy(a, b, load_sem.at[i]) for i, (a, b) in enumerate(loads)]
    for copy in copies:
        copy.start()

    barrier = pltpu.get_barrier_semaphore()

    def hello(device):
        pl.semaphore_signal(barrier, inc=1, device_id=device, device_id_type=MESH)

    for i in range(1, ZS):
        hello(at(x, z_peer(i)))
    for i in range(ZS):
        hello(at(cross, z_peer(i)))
    hello(at(pair, z))
    hello(at(far, z))
    own_in = jnp.logical_or(y == x, y == cross)
    source_x = jnp.where(own_in, x, pair)
    for s in range(8):
        @pl.when(jnp.logical_not(jnp.logical_and(own_in, t == s)))
        def _():
            hello((source_x * ZS + z, s))

    @pl.when(jnp.logical_and(z > 0, jnp.logical_or(x == 1, x == 2)))
    def _():
        hello((0, t))

    for b in range(2):
        vals[b, :, HD:] = jnp.ones((KEYS, HD), BF16)
    anchor_vals[:, HD:] = jnp.ones((BLK, HD), BF16)
    column = lax.broadcasted_iota(jnp.int32, (GROUP, PAD), 1)
    row = lax.broadcasted_iota(jnp.int32, (GROUP, PAD), 0)
    for g, gx in ((0, x), (1, cross)):
        for b, bx in ((0, x), (1, pair)):
            key_pos = bx * GROUP + z * ROWS + column
            seen = jnp.logical_and(column < ROWS, key_pos <= gx * GROUP + row)
            bias[g, b] = jnp.where(seen, 0.0, LOW).astype(F32)

    def push_own(src, dst, s_sem, r_sem):
        for i in range(1, ZS):
            there = z_peer(i)
            send(src(there), dst, s_sem, r_sem, at(x, there))

    def push_cross(src, dst, s_sem, r_sem):
        for i in range(ZS):
            there = z_peer(i)
            send(src(there), dst, s_sem, r_sem, at(cross, there))

    pair_device = at(pair, z)
    kv = [
        (k_hbm, keys.at[1, pl.ds(0, BLK)]),
        (v_hbm, vals.at[1, pl.ds(0, BLK), pl.ds(0, HD)]),
        (tk_hbm, keys.at[1, pl.ds(BLK, ROWS)]),
        (tv_hbm, vals.at[1, pl.ds(BLK, ROWS), pl.ds(0, HD)]),
    ]

    piece = 2 * BLK // (XS * ZS)
    in_keys = BLK // piece
    quarter_rows = ZS * piece

    def piece_of(i):
        return anchor.at[pl.ds(pl.multiple_of(i * piece, piece), piece)]

    def quarter(i):
        return anchor.at[pl.ds(pl.multiple_of(i * quarter_rows, quarter_rows), quarter_rows)]

    def greet():
        pl.semaphore_wait(barrier, 17 + jnp.where(own_in, 7, 8) + jnp.where(c == 0, 14, 0))

        @pl.when(c == 0)
        def _():
            def from_keys(i, carry):
                src = k_hbm.at[pl.ds(pl.multiple_of(i * piece, piece), piece)]
                send(src, piece_of(i), a_send.at[0], a_recv.at[0], (i, t))
                return carry

            def from_values(i, carry):
                src = v_hbm.at[pl.ds(pl.multiple_of((i - in_keys) * piece, piece), piece)]
                send(src, piece_of(i), a_send.at[0], a_recv.at[0], (i, t))
                return carry

            lax.fori_loop(1, in_keys, from_keys, 0)
            lax.fori_loop(in_keys, XS * ZS, from_values, 0)
            pltpu.make_async_copy(k_hbm.at[pl.ds(0, piece)], piece_of(0), load_sem.at[7]).start()

        push_own(lambda there: tq_hbm, tail_q.at[0, rows16(z)], q_send.at[0], q_recv.at[0])
        for i, (a, b) in enumerate(kv):
            send(a, b, kv_send.at[i], kv_recv.at[i], pair_device)

    def anchor_along_z():
        @pl.when(c > 0)
        def _():
            local_wait(piece_of(c), a_recv.at[0])

        @pl.when(c == 0)
        def _():
            local_wait(piece_of(0), load_sem.at[7])

        for i in range(1, ZS):
            send(piece_of(c), piece_of(c), a_send.at[1], a_recv.at[1], at(x, z_peer(i)))

    def anchor_along_x():
        local_wait(anchor.at[pl.ds(0, (ZS - 1) * piece)], a_recv.at[1])
        for dx in (pair, cross, far):
            send(quarter(x), quarter(x), a_send.at[2], a_recv.at[2], at(dx, z))

    def anchor_ready():
        local_wait(anchor.at[pl.ds(0, 3 * quarter_rows)], a_recv.at[2])
        anchor_vals[:, :HD] = anchor[BLK:, :]

    def columns_of(h):
        return pl.ds(pl.multiple_of(h * HD, HD), HD)

    short = pl.ds(0, GROUP - ROWS)

    def tail_block(b, g, j):
        first, second = columns_of(2 * j), columns_of(2 * j + 1)
        queries = jnp.concatenate([tail_q[g, :, first], tail_q[g, :, second]], axis=0)
        scores = lax.dot_general(queries, keys[b], NT, preferred_element_type=F32)
        seen = bias[g, b]
        last = scores[:, BLK:] + jnp.concatenate([seen, seen], axis=0)
        best, o = weighted(jnp.concatenate([scores[:, :BLK], last], axis=1), vals[b])
        return jnp.broadcast_to(best, (2 * GROUP, HD)), o

    def half_of(a):
        return pl.ds(pl.multiple_of(a * WIDE, HD), WIDE)

    def tail_finish(g, a, blocks):
        lane = lax.broadcasted_iota(jnp.int32, (GROUP, HD), 1)
        held = jnp.zeros((GROUP, HD), F32)
        for i, ((best_1, o_1), (best_2, o_2)) in enumerate(blocks):
            top = jnp.maximum(best_1, best_2)
            f_1, f_2 = jnp.exp2((best_1 - top) * C), jnp.exp2((best_2 - top) * C)
            num = o_1[:, :HD] * f_1 + o_2[:, :HD] * f_2
            den = o_1[:, HD:] * f_1 + o_2[:, HD:] * f_2
            normal = (num / den).astype(BF16)
            level = top * C + jnp.log(den) * LOG2E
            high = level.astype(BF16).astype(F32)
            middle = (level - high).astype(BF16).astype(F32)
            low = level - high - middle
            for k in range(2):
                h = 2 * i + k
                rows = slice(k * GROUP, (k + 1) * GROUP)
                part[g, :, pl.ds(pl.multiple_of(a * WIDE + h * HD, HD), HD)] = normal[rows]
                held = jnp.where(lane == h, high[rows], held)
                held = jnp.where(lane == h + 8, middle[rows], held)
                held = jnp.where(lane == h + 16, low[rows], held)
        part[g, :, pl.ds(pl.multiple_of(a * WIDE + HALF, HD), HD)] = held.astype(BF16)

    def tail_first():
        local_wait(tail_q.at[0, short], q_recv.at[0])
        for i in (3, 4, 5):
            copies[i].wait()
        send(tail_q.at[0], tail_q.at[1], q_send.at[1], q_recv.at[1], at(cross, z))

        def own_block(a, carry):
            for j in (2 * a, 2 * a + 1):
                best, o = tail_block(0, 0, j)
                tail_acc[j] = o
                tail_best[j] = best
            return carry

        lax.fori_loop(0, 2, own_block, 0)
        anchor_along_z()

    def tail():
        for i, (a, b) in enumerate(kv):
            local_wait(b, kv_recv.at[i])

        def group_0(a, carry):
            blocks = []
            for j in (2 * a, 2 * a + 1):
                other = tail_block(1, 0, j)
                blocks.append(((tail_best[j], tail_acc[j]), other))
            tail_finish(0, a, blocks)
            return carry

        lax.fori_loop(0, 2, group_0, 0)
        push_own(lambda there: part.at[0, rows16(there)], got.at[0, rows16(z)], p_send.at[0], p_recv.at[0])
        got[0, rows16(z), :] = part[0, rows16(z), :]
        local_wait(tail_q.at[1], q_recv.at[1])

        def group_1(a, carry):
            tail_finish(1, a, [(tail_block(0, 1, j), tail_block(1, 1, j)) for j in (2 * a, 2 * a + 1)])
            push_cross(
                lambda there: part.at[1, rows16(there), half_of(a)],
                got.at[1, rows16(z), half_of(a)],
                p_send.at[1 + a],
                p_recv.at[1 + a],
            )
            return carry

        lax.fori_loop(0, 2, group_1, 0)
        anchor_along_x()
        send(w_hbm, weight.at[1], w_send, w_recv, pair_device)

    def merge(a):
        if a == 0:
            local_wait(got.at[0, short], p_recv.at[0])
        local_wait(got.at[1, :, half_of(a)], p_recv.at[1 + a])
        levels = got[:, :, a * WIDE + HALF : (a + 1) * WIDE].astype(F32).reshape(2 * GROUP, HD)
        levels = levels + pltpu.roll(levels, HD - 8, 1) + pltpu.roll(levels, HD - 16, 1)
        levels = levels.reshape(2 * ZS, ROWS, HD)
        factors = jnp.exp2(levels - jnp.max(levels, axis=0, keepdims=True))
        factors = factors / jnp.sum(factors, axis=0, keepdims=True)
        for h in range(HEADS // 2):
            total = jnp.zeros((ROWS, HD), F32)
            for s in range(2 * ZS):
                g, i = s // ZS, s % ZS
                term = got[g, i * ROWS : (i + 1) * ROWS, a * WIDE + h * HD : a * WIDE + (h + 1) * HD].astype(F32)
                total = total + term * factors[s, :, h : h + 1]
            merged[a, 0, rows16(z), h * HD : (h + 1) * HD] = total.astype(BF16)
        mine = merged.at[a, 0, rows16(z)]
        push_cross(lambda there: mine, merged.at[a, 1, rows16(z)], m_send.at[a, 1], m_recv.at[a, 1])
        push_own(lambda there: mine, merged.at[a, 0, rows16(z)], m_send.at[a, 0], m_recv.at[a, 0])
        pltpu.make_async_copy(mine, attn_hbm.at[:, pl.ds(a * HALF, HALF)], out_sem.at[8 + a]).start()

    def project():
        copies[6].wait()
        local_wait(weight.at[1], w_recv)
        for a in range(2):
            local_wait(merged.at[a, 0, short], m_recv.at[a, 0])
            local_wait(merged.at[a, 1], m_recv.at[a, 1])
        for j, jx in ((1, pair), (0, x)):
            projected = jnp.zeros((2 * GROUP, 256), F32)
            for a in range(2):
                rows = merged[a].reshape(2 * GROUP, HALF)
                projected += jnp.dot(rows, weight[j, a * HALF : (a + 1) * HALF, :], preferred_element_type=F32)
            proj[j] = projected
            for g, gy in ((0, x), (1, cross)):
                for k in range(2):
                    src = proj.at[j, pl.ds(g * GROUP + k * 64, 64)]
                    to = 2 * gy + k
                    if j == 0:
                        @pl.when(to == t)
                        def _():
                            pieces[t] = src[...]

                        @pl.when(to != t)
                        def _():
                            send(src, pieces.at[t], r_send, r_recv, (c, to))
                    else:
                        send(src, pieces.at[t], r_send, r_recv, (jx * ZS + z, to))

    def own_head(h, carry):
        pl.when(h == GREET_AT)(greet)
        pl.when(h == FIRST_AT)(tail_first)
        pl.when(h == TAIL_AT)(tail)
        pl.when(h == MERGE_A_AT)(functools.partial(merge, 0))
        cols = columns_of(h)
        at_row = lax.broadcasted_iota(jnp.int32, (TILE, TILE), 0)
        at_col = lax.broadcasted_iota(jnp.int32, (TILE, TILE), 1)
        for i in range(BLK // TILE):
            rows, n = slice(i * TILE, (i + 1) * TILE), (i + 1) * TILE
            scores = lax.dot_general(q[rows, cols], keys[0, :n, :], NT, preferred_element_type=F32)
            last = jnp.where(at_col <= at_row, scores[:, n - TILE :], LOW)
            scores = jnp.concatenate([scores[:, : n - TILE], last], axis=1) if i else last
            best, o = weighted(scores, vals[0, :n, :])
            acc[h, rows, :] = o
            best_own[h, rows, :] = jnp.broadcast_to(best, (TILE, HD))
        return carry

    def anchor_head(h, carry):
        pl.when(h == MERGE_B_AT)(functools.partial(merge, 1))
        pl.when(h == PROJECT_AT)(project)
        cols = columns_of(h)
        for i in range(BLK // TILE):
            rows = slice(i * TILE, (i + 1) * TILE)
            scores = lax.dot_general(q[rows, cols], anchor[:BLK, :], NT, preferred_element_type=F32)
            best, o = weighted(scores, anchor_vals[...])
            best = jnp.where(c == 0, LOW, jnp.broadcast_to(best, (TILE, HD)))
            before = best_own[h, rows, :]
            top = jnp.maximum(before, best)
            f_own, f_anchor = jnp.exp2((before - top) * C), jnp.exp2((best - top) * C)
            own = acc[h, rows, :]
            num = own[:, :HD] * f_own + o[:, :HD] * f_anchor
            den = own[:, HD:] * f_own + o[:, HD:] * f_anchor
            out[rows, cols] = (num / den).astype(BF16)
        pltpu.make_async_copy(out.at[:, cols], out_hbm.at[:, cols], out_sem.at[h]).start()
        return carry

    if GREET_AT < 0:
        greet()
    for i in range(3):
        copies[i].wait()
    lax.fori_loop(0, HEADS, own_head, 0)
    anchor_ready()
    lax.fori_loop(0, HEADS, anchor_head, 0)

    for h in range(HEADS):
        cols = pl.ds(h * HD, HD)
        pltpu.make_async_copy(out.at[:, cols], out_hbm.at[:, cols], out_sem.at[h]).wait()
    for a in range(2):
        pltpu.make_async_copy(merged.at[a, 0, rows16(z)], attn_hbm.at[:, pl.ds(a * HALF, HALF)], out_sem.at[8 + a]).wait()
        local_wait(merged.at[a, 0, short], m_send.at[a, 0])
        local_wait(merged.at[a, 1], m_send.at[a, 1])
        local_wait(part.at[1, :, half_of(a)], p_send.at[1 + a])
    local_wait(part.at[0, short], p_send.at[0])
    local_wait(tail_q.at[0, short], q_send.at[0])
    local_wait(tail_q.at[1], q_send.at[1])
    for i, (a, b) in enumerate(kv):
        local_wait(b, kv_send.at[i])
    local_wait(weight.at[1], w_send)

    @pl.when(c == 0)
    def _():
        local_wait(anchor.at[pl.ds(0, (XS * ZS - 1) * piece)], a_send.at[0])

    local_wait(anchor.at[pl.ds(0, (ZS - 1) * piece)], a_send.at[1])
    local_wait(anchor.at[pl.ds(0, 3 * quarter_rows)], a_send.at[2])

    for sem in (r_recv, r_send):
        @pl.when(own_in)
        def _():
            local_wait(pieces.at[pl.ds(0, 7)], sem)

        @pl.when(jnp.logical_not(own_in))
        def _():
            local_wait(pieces, sem)

    total = pieces[0]
    for i in range(1, 8):
        total = total + pieces[i]
    result[...] = total
    last = pltpu.make_async_copy(result, proj_hbm, out_sem.at[10])
    last.start()
    last.wait()


def on_device(*args):
    width = HEADS * HD
    dma = pltpu.SemaphoreType.DMA
    shapes = (
        jax.ShapeDtypeStruct((BLK, width), BF16),
        jax.ShapeDtypeStruct((ROWS, width), BF16),
        jax.ShapeDtypeStruct((64, 256), F32),
    )
    results = pl.pallas_call(
        kernel,
        out_shape=shapes,
        in_specs=[pl.BlockSpec(memory_space=pl.ANY)] * 7,
        out_specs=[pl.BlockSpec(memory_space=pl.ANY)] * 3,
        scratch_shapes=[
            pltpu.VMEM((BLK, width), BF16),
            pltpu.VMEM((2, KEYS, HD), BF16),
            pltpu.VMEM((2, KEYS, 2 * HD), BF16),
            pltpu.VMEM((2 * BLK, HD), BF16),
            pltpu.VMEM((BLK, 2 * HD), BF16),
            pltpu.VMEM((HEADS, BLK, 2 * HD), F32),
            pltpu.VMEM((HEADS, BLK, HD), F32),
            pltpu.VMEM((BLK, width), BF16),
            pltpu.VMEM((2, GROUP, width), BF16),
            pltpu.VMEM((2, 2, GROUP, PAD), F32),
            pltpu.VMEM((HEADS // 2, 2 * GROUP, 2 * HD), F32),
            pltpu.VMEM((HEADS // 2, 2 * GROUP, HD), F32),
            pltpu.VMEM((2, GROUP, 2 * WIDE), BF16),
            pltpu.VMEM((2, GROUP, 2 * WIDE), BF16),
            pltpu.VMEM((2, 2, GROUP, HALF), BF16),
            pltpu.VMEM((2, width, 256), BF16),
            pltpu.VMEM((2, 2 * GROUP, 256), F32),
            pltpu.VMEM((8, 64, 256), F32),
            pltpu.VMEM((64, 256), F32),
            dma((8,)),
            dma((11,)),
            dma((2,)), dma((2,)),
            dma((4,)), dma((4,)),
            dma((3,)), dma((3,)),
            dma((3,)), dma((3,)),
            dma((2, 2)), dma((2, 2)),
            dma, dma,
            dma, dma,
        ],
        compiler_params=pltpu.CompilerParams(
            collective_id=0, has_side_effects=True, vmem_limit_bytes=56 * 2**20
        ),
    )(*args)
    return pl.pallas_call(
        copy_out,
        out_shape=shapes,
        in_specs=[pl.BlockSpec(memory_space=pltpu.HBM)] * 3,
        out_specs=[pl.BlockSpec(memory_space=pltpu.HBM)] * 3,
        scratch_shapes=[pltpu.VMEM(s.shape, s.dtype) for s in shapes] + [dma((2, CHUNKS + 2))],
        compiler_params=pltpu.CompilerParams(vmem_limit_bytes=56 * 2**20),
    )(*results)


def solution(mesh):
    placed = (P("ctx", "tp"),) * 6 + (P("tp", "ctx"),)
    return jax.shard_map(
        on_device,
        mesh=mesh,
        in_specs=placed,
        out_specs=(P("ctx", "tp"), P("ctx", "tp"), P("tp", "ctx")),
        check_vma=False,
    )
```

```python
import functools

import jax
import jax.numpy as jnp
from jax import lax
from jax.experimental import pallas as pl
from jax.experimental.pallas import tpu as pltpu
from jax.sharding import PartitionSpec as P

HD = 128
HEADS = 8
BLK = 1024
ROWS = 16
GROUP = 128
XS, ZS, YS = 4, 8, 4
TILE = 256
PAD = 128
KEYS = BLK + PAD
HALF = HEADS // 2 * HD
WIDE = HALF + HD
LOG2E = 1.4426950408889634
C = LOG2E * HD ** (-0.5)
LOW = -1e30
CHUNKS = 8
GREET_AT, FIRST_AT, TAIL_AT, MERGE_A_AT = 0, 4, 5, 7
MERGE_B_AT, PROJECT_AT = 1, 5
NT = (((1,), (1,)), ((), ()))
MESH = pl.DeviceIdType.MESH
F32, BF16 = jnp.float32, jnp.bfloat16


def local_wait(ref, sem):
    pltpu.make_async_copy(ref, ref, sem).wait()


def weighted(scores, values):
    best = jnp.max(scores, axis=1, keepdims=True)
    weights = jnp.exp2((scores - best) * C).astype(BF16)
    return best, jnp.dot(weights, values, preferred_element_type=F32)


def copy_out(*refs):
    sources, results, buffers, sems = refs[:3], refs[3:6], refs[6:9], refs[9]
    step = BLK // CHUNKS
    parts = [(i, pl.ds(0, results[i].shape[0])) for i in (1, 2)]
    parts = [(0, pl.ds(i * step, step)) for i in range(CHUNKS)] + parts
    loads = [pltpu.make_async_copy(sources[i].at[s], buffers[i].at[s], sems.at[0, n]) for n, (i, s) in enumerate(parts)]
    stores = [pltpu.make_async_copy(buffers[i].at[s], results[i].at[s], sems.at[1, n]) for n, (i, s) in enumerate(parts)]
    for copy in loads:
        copy.start()
    for load, store in zip(loads, stores):
        load.wait()
        store.start()
    for copy in stores:
        copy.wait()


def kernel(
    q_hbm, k_hbm, v_hbm, tq_hbm, tk_hbm, tv_hbm, w_hbm,
    out_hbm, attn_hbm, proj_hbm,
    q, keys, vals, anchor, anchor_vals, acc, best_own, out,
    tail_q, bias, tail_acc, tail_best, part, got, merged, weight, proj, pieces, result,
    load_sem, out_sem, q_send, q_recv, kv_send, kv_recv, a_send, a_recv,
    p_send, p_recv, m_send, m_recv, w_send, w_recv, r_send, r_recv,
):
    c, t = lax.axis_index("ctx"), lax.axis_index("tp")
    x, z, y = c // ZS, c % ZS, t // 2
    pair = x + 1 - 2 * (x % 2)
    cross = XS - 1 - x
    far = (x + 2) % XS

    def at(dx, dz):
        return (dx * ZS + dz, t)

    def z_peer(i):
        return (z + i) % ZS

    def send(src, dst, s_sem, r_sem, device):
        pltpu.make_async_remote_copy(
            src_ref=src, dst_ref=dst, send_sem=s_sem, recv_sem=r_sem, device_id=device, device_id_type=MESH
        ).start()

    def rows16(i):
        return pl.ds(pl.multiple_of(i * ROWS, ROWS), ROWS)

    loads = [
        (k_hbm, keys.at[0, pl.ds(0, BLK)]),
        (v_hbm, vals.at[0, pl.ds(0, BLK), pl.ds(0, HD)]),
        (q_hbm, q),
        (tk_hbm, keys.at[0, pl.ds(BLK, ROWS)]),
        (tv_hbm, vals.at[0, pl.ds(BLK, ROWS), pl.ds(0, HD)]),
        (tq_hbm, tail_q.at[0, rows16(z)]),
        (w_hbm, weight.at[0]),
    ]
    for b in range(2):
        keys[b, BLK:, :] = jnp.zeros((PAD, HD), BF16)
        vals[b, BLK:, :HD] = jnp.zeros((PAD, HD), BF16)
    copies = [pltpu.make_async_copy(a, b, load_sem.at[i]) for i, (a, b) in enumerate(loads)]
    for copy in copies:
        copy.start()

    barrier = pltpu.get_barrier_semaphore()

    def hello(device):
        pl.semaphore_signal(barrier, inc=1, device_id=device, device_id_type=MESH)

    for i in range(1, ZS):
        hello(at(x, z_peer(i)))
    for i in range(ZS):
        hello(at(cross, z_peer(i)))
    hello(at(pair, z))
    hello(at(far, z))
    own_in = jnp.logical_or(y == x, y == cross)
    source_x = jnp.where(own_in, x, pair)
    for s in range(8):
        @pl.when(jnp.logical_not(jnp.logical_and(own_in, t == s)))
        def _():
            hello((source_x * ZS + z, s))

    @pl.when(jnp.logical_and(z > 0, jnp.logical_or(x == 1, x == 2)))
    def _():
        hello((0, t))

    for b in range(2):
        vals[b, :, HD:] = jnp.ones((KEYS, HD), BF16)
    anchor_vals[:, HD:] = jnp.ones((BLK, HD), BF16)
    column = lax.broadcasted_iota(jnp.int32, (GROUP, PAD), 1)
    row = lax.broadcasted_iota(jnp.int32, (GROUP, PAD), 0)
    for g, gx in ((0, x), (1, cross)):
        for b, bx in ((0, x), (1, pair)):
            key_pos = bx * GROUP + z * ROWS + column
            seen = jnp.logical_and(column < ROWS, key_pos <= gx * GROUP + row)
            bias[g, b] = jnp.where(seen, 0.0, LOW).astype(F32)

    def push_own(src, dst, s_sem, r_sem):
        for i in range(1, ZS):
            there = z_peer(i)
            send(src(there), dst, s_sem, r_sem, at(x, there))

    def push_cross(src, dst, s_sem, r_sem):
        for i in range(ZS):
            there = z_peer(i)
            send(src(there), dst, s_sem, r_sem, at(cross, there))

    pair_device = at(pair, z)
    kv = [
        (k_hbm, keys.at[1, pl.ds(0, BLK)]),
        (v_hbm, vals.at[1, pl.ds(0, BLK), pl.ds(0, HD)]),
        (tk_hbm, keys.at[1, pl.ds(BLK, ROWS)]),
        (tv_hbm, vals.at[1, pl.ds(BLK, ROWS), pl.ds(0, HD)]),
    ]

    piece = 2 * BLK // (XS * ZS)
    in_keys = BLK // piece
    quarter_rows = ZS * piece

    def piece_of(i):
        return anchor.at[pl.ds(pl.multiple_of(i * piece, piece), piece)]

    def quarter(i):
        return anchor.at[pl.ds(pl.multiple_of(i * quarter_rows, quarter_rows), quarter_rows)]

    def greet():
        pl.semaphore_wait(barrier, 17 + jnp.where(own_in, 7, 8) + jnp.where(c == 0, 14, 0))

        @pl.when(c == 0)
        def _():
            def from_keys(i, carry):
                src = k_hbm.at[pl.ds(pl.multiple_of(i * piece, piece), piece)]
                send(src, piece_of(i), a_send.at[0], a_recv.at[0], (i, t))
                return carry

            def from_values(i, carry):
                src = v_hbm.at[pl.ds(pl.multiple_of((i - in_keys) * piece, piece), piece)]
                send(src, piece_of(i), a_send.at[0], a_recv.at[0], (i, t))
                return carry

            lax.fori_loop(1, in_keys, from_keys, 0)
            lax.fori_loop(in_keys, XS * ZS, from_values, 0)
            pltpu.make_async_copy(k_hbm.at[pl.ds(0, piece)], piece_of(0), load_sem.at[7]).start()

        push_own(lambda there: tq_hbm, tail_q.at[0, rows16(z)], q_send.at[0], q_recv.at[0])
        for i, (a, b) in enumerate(kv):
            send(a, b, kv_send.at[i], kv_recv.at[i], pair_device)

    def anchor_along_z():
        @pl.when(c > 0)
        def _():
            local_wait(piece_of(c), a_recv.at[0])

        @pl.when(c == 0)
        def _():
            local_wait(piece_of(0), load_sem.at[7])

        for i in range(1, ZS):
            send(piece_of(c), piece_of(c), a_send.at[1], a_recv.at[1], at(x, z_peer(i)))

    def anchor_along_x():
        local_wait(anchor.at[pl.ds(0, (ZS - 1) * piece)], a_recv.at[1])
        for dx in (pair, cross, far):
            send(quarter(x), quarter(x), a_send.at[2], a_recv.at[2], at(dx, z))

    def anchor_ready():
        local_wait(anchor.at[pl.ds(0, 3 * quarter_rows)], a_recv.at[2])
        anchor_vals[:, :HD] = anchor[BLK:, :]

    def columns_of(h):
        return pl.ds(pl.multiple_of(h * HD, HD), HD)

    short = pl.ds(0, GROUP - ROWS)

    def tail_block(b, g, j):
        first, second = columns_of(2 * j), columns_of(2 * j + 1)
        queries = jnp.concatenate([tail_q[g, :, first], tail_q[g, :, second]], axis=0)
        scores = lax.dot_general(queries, keys[b], NT, preferred_element_type=F32)
        seen = bias[g, b]
        last = scores[:, BLK:] + jnp.concatenate([seen, seen], axis=0)
        best, o = weighted(jnp.concatenate([scores[:, :BLK], last], axis=1), vals[b])
        return jnp.broadcast_to(best, (2 * GROUP, HD)), o

    def half_of(a):
        return pl.ds(pl.multiple_of(a * WIDE, HD), WIDE)

    def tail_finish(g, a, blocks):
        lane = lax.broadcasted_iota(jnp.int32, (GROUP, HD), 1)
        held = jnp.zeros((GROUP, HD), F32)
        for i, ((best_1, o_1), (best_2, o_2)) in enumerate(blocks):
            top = jnp.maximum(best_1, best_2)
            f_1, f_2 = jnp.exp2((best_1 - top) * C), jnp.exp2((best_2 - top) * C)
            num = o_1[:, :HD] * f_1 + o_2[:, :HD] * f_2
            den = o_1[:, HD:] * f_1 + o_2[:, HD:] * f_2
            normal = (num / den).astype(BF16)
            level = top * C + jnp.log(den) * LOG2E
            high = level.astype(BF16).astype(F32)
            middle = (level - high).astype(BF16).astype(F32)
            low = level - high - middle
            for k in range(2):
                h = 2 * i + k
                rows = slice(k * GROUP, (k + 1) * GROUP)
                part[g, :, pl.ds(pl.multiple_of(a * WIDE + h * HD, HD), HD)] = normal[rows]
                held = jnp.where(lane == h, high[rows], held)
                held = jnp.where(lane == h + 8, middle[rows], held)
                held = jnp.where(lane == h + 16, low[rows], held)
        part[g, :, pl.ds(pl.multiple_of(a * WIDE + HALF, HD), HD)] = held.astype(BF16)

    def tail_first():
        local_wait(tail_q.at[0, short], q_recv.at[0])
        for i in (3, 4, 5):
            copies[i].wait()
        send(tail_q.at[0], tail_q.at[1], q_send.at[1], q_recv.at[1], at(cross, z))

        def own_block(a, carry):
            for j in (2 * a, 2 * a + 1):
                best, o = tail_block(0, 0, j)
                tail_acc[j] = o
                tail_best[j] = best
            return carry

        lax.fori_loop(0, 2, own_block, 0, unroll=True)
        anchor_along_z()

    def tail():
        for i, (a, b) in enumerate(kv):
            local_wait(b, kv_recv.at[i])

        def group_0(a, carry):
            blocks = []
            for j in (2 * a, 2 * a + 1):
                other = tail_block(1, 0, j)
                blocks.append(((tail_best[j], tail_acc[j]), other))
            tail_finish(0, a, blocks)
            return carry

        lax.fori_loop(0, 2, group_0, 0, unroll=True)
        push_own(lambda there: part.at[0, rows16(there)], got.at[0, rows16(z)], p_send.at[0], p_recv.at[0])
        got[0, rows16(z), :] = part[0, rows16(z), :]
        local_wait(tail_q.at[1], q_recv.at[1])

        def group_1(a, carry):
            tail_finish(1, a, [(tail_block(0, 1, j), tail_block(1, 1, j)) for j in (2 * a, 2 * a + 1)])
            push_cross(
                lambda there: part.at[1, rows16(there), half_of(a)],
                got.at[1, rows16(z), half_of(a)],
                p_send.at[1 + a],
                p_recv.at[1 + a],
            )
            return carry

        lax.fori_loop(0, 2, group_1, 0)
        anchor_along_x()
        send(w_hbm, weight.at[1], w_send, w_recv, pair_device)

    def merge(a):
        if a == 0:
            local_wait(got.at[0, short], p_recv.at[0])
        local_wait(got.at[1, :, half_of(a)], p_recv.at[1 + a])
        levels = got[:, :, a * WIDE + HALF : (a + 1) * WIDE].astype(F32).reshape(2 * GROUP, HD)
        levels = levels + pltpu.roll(levels, HD - 8, 1) + pltpu.roll(levels, HD - 16, 1)
        levels = levels.reshape(2 * ZS, ROWS, HD)
        factors = jnp.exp2(levels - jnp.max(levels, axis=0, keepdims=True))
        factors = factors / jnp.sum(factors, axis=0, keepdims=True)
        for h in range(HEADS // 2):
            total = jnp.zeros((ROWS, HD), F32)
            for s in range(2 * ZS):
                g, i = s // ZS, s % ZS
                term = got[g, i * ROWS : (i + 1) * ROWS, a * WIDE + h * HD : a * WIDE + (h + 1) * HD].astype(F32)
                total = total + term * factors[s, :, h : h + 1]
            merged[a, 0, rows16(z), h * HD : (h + 1) * HD] = total.astype(BF16)
        mine = merged.at[a, 0, rows16(z)]
        push_cross(lambda there: mine, merged.at[a, 1, rows16(z)], m_send.at[a, 1], m_recv.at[a, 1])
        push_own(lambda there: mine, merged.at[a, 0, rows16(z)], m_send.at[a, 0], m_recv.at[a, 0])
        pltpu.make_async_copy(mine, attn_hbm.at[:, pl.ds(a * HALF, HALF)], out_sem.at[8 + a]).start()

    def project():
        copies[6].wait()
        local_wait(weight.at[1], w_recv)
        for a in range(2):
            local_wait(merged.at[a, 0, short], m_recv.at[a, 0])
            local_wait(merged.at[a, 1], m_recv.at[a, 1])
        for j, jx in ((1, pair), (0, x)):
            projected = jnp.zeros((2 * GROUP, 256), F32)
            for a in range(2):
                rows = merged[a].reshape(2 * GROUP, HALF)
                projected += jnp.dot(rows, weight[j, a * HALF : (a + 1) * HALF, :], preferred_element_type=F32)
            proj[j] = projected.astype(BF16)
            for g, gy in ((0, x), (1, cross)):
                for k in range(2):
                    src = proj.at[j, pl.ds(g * GROUP + k * 64, 64)]
                    to = 2 * gy + k
                    if j == 0:
                        @pl.when(to == t)
                        def _():
                            pieces[t] = src[...]

                        @pl.when(to != t)
                        def _():
                            send(src, pieces.at[t], r_send, r_recv, (c, to))
                    else:
                        send(src, pieces.at[t], r_send, r_recv, (jx * ZS + z, to))

    def own_head(h, carry):
        pl.when(h == GREET_AT)(greet)
        pl.when(h == FIRST_AT)(tail_first)
        pl.when(h == TAIL_AT)(tail)
        pl.when(h == MERGE_A_AT)(functools.partial(merge, 0))
        cols = columns_of(h)
        at_row = lax.broadcasted_iota(jnp.int32, (TILE, TILE), 0)
        at_col = lax.broadcasted_iota(jnp.int32, (TILE, TILE), 1)
        for i in range(BLK // TILE):
            rows, n = slice(i * TILE, (i + 1) * TILE), (i + 1) * TILE
            scores = lax.dot_general(q[rows, cols], keys[0, :n, :], NT, preferred_element_type=F32)
            last = jnp.where(at_col <= at_row, scores[:, n - TILE :], LOW)
            scores = jnp.concatenate([scores[:, : n - TILE], last], axis=1) if i else last
            best, o = weighted(scores, vals[0, :n, :])
            acc[h, rows, :] = o
            best_own[h, rows, :] = jnp.broadcast_to(best, (TILE, HD))
        return carry

    def anchor_head(h, carry):
        pl.when(h == MERGE_B_AT)(functools.partial(merge, 1))
        pl.when(h == PROJECT_AT)(project)
        cols = columns_of(h)
        for i in range(BLK // TILE):
            rows = slice(i * TILE, (i + 1) * TILE)
            scores = lax.dot_general(q[rows, cols], anchor[:BLK, :], NT, preferred_element_type=F32)
            best, o = weighted(scores, anchor_vals[...])
            best = jnp.where(c == 0, LOW, jnp.broadcast_to(best, (TILE, HD)))
            before = best_own[h, rows, :]
            top = jnp.maximum(before, best)
            f_own, f_anchor = jnp.exp2((before - top) * C), jnp.exp2((best - top) * C)
            own = acc[h, rows, :]
            num = own[:, :HD] * f_own + o[:, :HD] * f_anchor
            den = own[:, HD:] * f_own + o[:, HD:] * f_anchor
            out[rows, cols] = (num / den).astype(BF16)
        pltpu.make_async_copy(out.at[:, cols], out_hbm.at[:, cols], out_sem.at[h]).start()
        return carry

    if GREET_AT < 0:
        greet()
    for i in range(3):
        copies[i].wait()
    lax.fori_loop(0, HEADS, own_head, 0)
    anchor_ready()
    lax.fori_loop(0, HEADS, anchor_head, 0)

    for h in range(HEADS):
        cols = pl.ds(h * HD, HD)
        pltpu.make_async_copy(out.at[:, cols], out_hbm.at[:, cols], out_sem.at[h]).wait()
    for a in range(2):
        pltpu.make_async_copy(merged.at[a, 0, rows16(z)], attn_hbm.at[:, pl.ds(a * HALF, HALF)], out_sem.at[8 + a]).wait()
        local_wait(merged.at[a, 0, short], m_send.at[a, 0])
        local_wait(merged.at[a, 1], m_send.at[a, 1])
        local_wait(part.at[1, :, half_of(a)], p_send.at[1 + a])
    local_wait(part.at[0, short], p_send.at[0])
    local_wait(tail_q.at[0, short], q_send.at[0])
    local_wait(tail_q.at[1], q_send.at[1])
    for i, (a, b) in enumerate(kv):
        local_wait(b, kv_send.at[i])
    local_wait(weight.at[1], w_send)

    @pl.when(c == 0)
    def _():
        local_wait(anchor.at[pl.ds(0, (XS * ZS - 1) * piece)], a_send.at[0])

    local_wait(anchor.at[pl.ds(0, (ZS - 1) * piece)], a_send.at[1])
    local_wait(anchor.at[pl.ds(0, 3 * quarter_rows)], a_send.at[2])

    for sem in (r_recv, r_send):
        @pl.when(own_in)
        def _():
            local_wait(pieces.at[pl.ds(0, 7)], sem)

        @pl.when(jnp.logical_not(own_in))
        def _():
            local_wait(pieces, sem)

    total = pieces[0].astype(F32)
    for i in range(1, 8):
        total = total + pieces[i].astype(F32)
    result[...] = total
    last = pltpu.make_async_copy(result, proj_hbm, out_sem.at[10])
    last.start()
    last.wait()


def on_device(*args):
    width = HEADS * HD
    dma = pltpu.SemaphoreType.DMA
    shapes = (
        jax.ShapeDtypeStruct((BLK, width), BF16),
        jax.ShapeDtypeStruct((ROWS, width), BF16),
        jax.ShapeDtypeStruct((64, 256), F32),
    )
    results = pl.pallas_call(
        kernel,
        out_shape=shapes,
        in_specs=[pl.BlockSpec(memory_space=pl.ANY)] * 7,
        out_specs=[pl.BlockSpec(memory_space=pl.ANY)] * 3,
        scratch_shapes=[
            pltpu.VMEM((BLK, width), BF16),
            pltpu.VMEM((2, KEYS, HD), BF16),
            pltpu.VMEM((2, KEYS, 2 * HD), BF16),
            pltpu.VMEM((2 * BLK, HD), BF16),
            pltpu.VMEM((BLK, 2 * HD), BF16),
            pltpu.VMEM((HEADS, BLK, 2 * HD), F32),
            pltpu.VMEM((HEADS, BLK, HD), F32),
            pltpu.VMEM((BLK, width), BF16),
            pltpu.VMEM((2, GROUP, width), BF16),
            pltpu.VMEM((2, 2, GROUP, PAD), F32),
            pltpu.VMEM((HEADS // 2, 2 * GROUP, 2 * HD), F32),
            pltpu.VMEM((HEADS // 2, 2 * GROUP, HD), F32),
            pltpu.VMEM((2, GROUP, 2 * WIDE), BF16),
            pltpu.VMEM((2, GROUP, 2 * WIDE), BF16),
            pltpu.VMEM((2, 2, GROUP, HALF), BF16),
            pltpu.VMEM((2, width, 256), BF16),
            pltpu.VMEM((2, 2 * GROUP, 256), BF16),
            pltpu.VMEM((8, 64, 256), BF16),
            pltpu.VMEM((64, 256), F32),
            dma((8,)),
            dma((11,)),
            dma((2,)), dma((2,)),
            dma((4,)), dma((4,)),
            dma((3,)), dma((3,)),
            dma((3,)), dma((3,)),
            dma((2, 2)), dma((2, 2)),
            dma, dma,
            dma, dma,
        ],
        compiler_params=pltpu.CompilerParams(
            collective_id=0, has_side_effects=True, vmem_limit_bytes=56 * 2**20
        ),
    )(*args)
    return pl.pallas_call(
        copy_out,
        out_shape=shapes,
        in_specs=[pl.BlockSpec(memory_space=pltpu.HBM)] * 3,
        out_specs=[pl.BlockSpec(memory_space=pltpu.HBM)] * 3,
        scratch_shapes=[pltpu.VMEM(s.shape, s.dtype) for s in shapes] + [dma((2, CHUNKS + 2))],
        compiler_params=pltpu.CompilerParams(vmem_limit_bytes=56 * 2**20),
    )(*results)


def solution(mesh):
    placed = (P("ctx", "tp"),) * 6 + (P("tp", "ctx"),)
    return jax.shard_map(
        on_device,
        mesh=mesh,
        in_specs=placed,
        out_specs=(P("ctx", "tp"), P("ctx", "tp"), P("tp", "ctx")),
        check_vma=False,
    )
```
